32 devices in a mesh: grp: 4 (over y, x), dom: 8 (over z, core).
Axes of the slice: x: 2, y: 2, z: 4, core: 2. Of those that a mesh axis runs over, the one named last changes fastest.
Arguments:
- entities: float32 [8192, 256], P(('grp', 'dom')), may hold values from -1.5 to 1.5
- relations: float32 [1920, 256], replicated, may hold values from -3.5 to 3.5
- edge_src: int32 [32, 4, 1024], P(('grp', 'dom')), may hold values from 0 to 255
- edge_rel: int32 [32, 4, 1024], P(('grp', 'dom')), may hold values from 0 to 1919
- edge_dst: int32 [32, 4, 1024], P(('grp', 'dom')), may hold values from 0 to 255
- negatives: int32 [32, 4, 8, 512], P(('grp', 'dom')), may hold values from 0 to 255
- plan: int32 [4], replicated, may hold values from 1 to 7, as said below
- edge_counts: int32 [32, 4], P(('grp', 'dom')), may hold values from 1 to 1024, as said below
Outputs:
- entity_grads: float32 [8192, 256], P(('grp', 'dom'))
- relation_grads: float32 [1920, 256], P('dom')
The draws below stay inside these ranges and needn't reach their ends.
Inputs may be any that keep to these rules, and one draw needn't show every extreme that they name: `plan`: 4 distinct values, one of them 8 - 1. `edge_counts`: in every round some partition has 1024 edges.
All inputs are finite; a program needn't handle non-finite values.
Results may differ from the reference program's by a relative error of at most 0.0052.
Values may be sent and summed in bfloat16 or wider, within the bound.
A program may use at most 128 MiB of HBM per device.

```python
import math
import jax
import jax.numpy as jnp
import numpy as np
from jax import lax

D = 256
ENT_DEV = 256
BATCH = 128
NEG = 512
BATCHES = 8
ROUNDS = 4
GROUP = 8
PARTITIONS = 32
ENTITIES = 8192
EDGE_CAP = 1024
REL = 1920


def draw_plan(key, part):
    first_key = jax.random.fold_in(key, 11)
    second_key = jax.random.fold_in(key, 12)
    others = jax.random.permutation(first_key, GROUP - 2)[:ROUNDS - 1] + 1
    codes = jnp.concatenate([others.astype(jnp.int32), jnp.full((1,), GROUP - 1, jnp.int32)])
    return jax.random.permutation(second_key, codes).astype(jnp.int32)


def draw_edge_counts(key, part):
    level_key = jax.random.fold_in(key, 21)
    trim_key = jax.random.fold_in(key, 22)
    pick_key = jax.random.fold_in(key, 23)
    levels = jax.random.randint(level_key, (PARTITIONS, ROUNDS), 0, 3)
    divisor = jnp.where(levels == 0, 1, jnp.where(levels == 1, 2, 4)).astype(jnp.int32)
    ceiling = jnp.int32(EDGE_CAP) // divisor
    trimmed = ceiling - jax.random.randint(trim_key, (PARTITIONS, ROUNDS), 0, ceiling // 4 + 1)
    busiest = jax.random.randint(pick_key, (ROUNDS,), 0, PARTITIONS)
    rows_index = jnp.arange(PARTITIONS, dtype=jnp.int32)[:, None]
    return jnp.where(rows_index == busiest[None, :], EDGE_CAP, trimmed).astype(jnp.int32)


def set_ends(array, rng, low, largest):
    longest = array.shape.index(max(array.shape))
    spots = []
    for shift in (0, 1):
        where = [jax.random.randint(jax.random.fold_in(rng, axis), (), 0, length) for axis, length in enumerate(array.shape)]
        where[longest] = (where[longest] + shift) % array.shape[longest]
        spots.append(tuple(where))
    return array.at[spots[0]].set(low).at[spots[1]].set(largest)


def block_scale(stream_key, shape, split, least, largest):
    loudness, own = 1.0, jax.random.fold_in(stream_key, 6)
    for dim, blocks in split:
        draws = jnp.exp(jax.random.uniform(jax.random.fold_in(own, dim), (blocks,), jnp.float32, least / len(split), largest / len(split)))
        loudness = loudness * jnp.repeat(draws, shape[dim] // blocks).reshape([-1 if axis == dim else 1 for axis in range(len(shape))])
    return loudness


def rank_bounds(amount, slope):
    loads = [(1 << 20) // math.isqrt(grade ** slope) + 1 for grade in range(1, amount + 1)]
    width = 1 + sum(loads) // (1 << 30)
    return np.cumsum(np.array([max(1, weight // width) for weight in loads]))


def skewed_ids(stream_key, dims, amount, skew):
    grid = rank_bounds(amount, skew)
    pick = jax.random.randint(jax.random.fold_in(stream_key, 1), dims, 0, int(grid[amount - 1]))
    grade = jnp.searchsorted(jnp.asarray(grid, jnp.int32), pick, side="right")
    return jax.random.permutation(jax.random.fold_in(stream_key, 2), amount)[grade].astype(jnp.int32)


def bell_draw(own_key, dims, scale, most, cuts=(), kind=jnp.bfloat16):
    level = block_scale(own_key, dims, cuts, -0.22, 0.18) if cuts else 1.0
    array = jax.random.normal(own_key, dims, jnp.float32) * scale * level
    return jnp.minimum(jnp.maximum(array, -most), most).astype(kind)


def setup_inputs(seed: int = 0) -> dict:
    keys = jax.random.split(jax.random.key(seed), 9)
    return {
        "entities": bell_draw(keys[0], (ENTITIES, D), 0.25, 1.5, ((0, 32),), jnp.float32),
        "relations": bell_draw(keys[1], (REL, D), 0.7, 3.5, (), jnp.float32),
        "edge_src": set_ends(jax.random.randint(keys[2], (PARTITIONS, ROUNDS, EDGE_CAP), 0, ENT_DEV), jax.random.fold_in(keys[2], 1), 0, ENT_DEV - 1).astype(jnp.int32),
        "edge_rel": set_ends(skewed_ids(keys[3], (PARTITIONS, ROUNDS, EDGE_CAP), REL, 1), jax.random.fold_in(keys[3], 3), 0, REL - 1).astype(jnp.int32),
        "edge_dst": set_ends(jax.random.randint(keys[4], (PARTITIONS, ROUNDS, EDGE_CAP), 0, ENT_DEV), jax.random.fold_in(keys[4], 1), 0, ENT_DEV - 1).astype(jnp.int32),
        "negatives": set_ends(jax.random.randint(keys[5], (PARTITIONS, ROUNDS, BATCHES, NEG), 0, ENT_DEV), jax.random.fold_in(keys[5], 1), 0, ENT_DEV - 1).astype(jnp.int32),
        "plan": draw_plan(jax.random.fold_in(keys[8], 71), 0),
        "edge_counts": draw_edge_counts(jax.random.fold_in(keys[8], 71), 0),
    }


step_size = 0.1


def complex_product(factor, second):
    halfway = factor.shape[-1] // 2
    first_re, first_im = factor[..., :halfway], factor[..., halfway:]
    second_re, second_im = second[..., :halfway], second[..., halfway:]
    return jnp.concatenate([first_re * second_re - first_im * second_im, first_re * second_im + first_im * second_re], axis=-1)


def conj_product(gradient, second):
    halfway = gradient.shape[-1] // 2
    grad_re, grad_im = gradient[..., :halfway], gradient[..., halfway:]
    second_re, second_im = second[..., :halfway], second[..., halfway:]
    return jnp.concatenate([grad_re * second_re + grad_im * second_im, grad_im * second_re - grad_re * second_im], axis=-1)


def batch_terms(src_block, dst_block, rel_table, src_ids, rel_ids, dst_ids, neg_ids, live_edges):
    source = jnp.take(src_block, src_ids, axis=0).astype(jnp.float32)
    relation = jnp.take(rel_table, rel_ids, axis=0).astype(jnp.float32)
    product = complex_product(source, relation).astype(jnp.bfloat16)
    target = jnp.take(dst_block, dst_ids, axis=0)
    sampled = jnp.take(dst_block, neg_ids, axis=0)
    positive = jnp.sum(product.astype(jnp.float32) * target.astype(jnp.float32), axis=1)
    negative = jnp.dot(product, sampled.T, preferred_element_type=jnp.float32)
    weights = live_edges[:, None] * jax.nn.sigmoid(negative - positive[:, None]) / sampled.shape[0]
    weights_bf = weights.astype(jnp.bfloat16)
    pull_back = -jnp.sum(weights, axis=1)
    grad_product = jnp.dot(weights_bf, sampled, preferred_element_type=jnp.float32) + pull_back[:, None] * target.astype(jnp.float32)
    grad_sampled = jnp.dot(weights_bf.T, product, preferred_element_type=jnp.float32)
    grad_target = pull_back[:, None] * product.astype(jnp.float32)
    grad_source = conj_product(grad_product, relation)
    grad_relation = conj_product(grad_product, source)
    return grad_source, grad_relation, grad_target, grad_sampled


def reference(entities, relations, edge_src, edge_rel, edge_dst, negatives, plan, edge_counts):
    rel_table = relations.astype(jnp.bfloat16)
    blocks = entities.reshape(PARTITIONS, ENT_DEV, D)
    grad_total = jnp.zeros((PARTITIONS, ENT_DEV, D), jnp.float32)
    rel_grads = jnp.zeros((REL, D), jnp.float32)
    members = jnp.arange(PARTITIONS, dtype=jnp.int32)
    for round_index in range(ROUNDS):
        partner_mask = plan[round_index]
        partner = (members // GROUP) * GROUP + jnp.bitwise_xor(members % GROUP, partner_mask)
        blocks_bf = blocks.astype(jnp.bfloat16)

        def per_partition(rel_carry, member):
            mate = partner[member]
            own_bf = blocks_bf[member]
            mate_bf = blocks_bf[mate]
            edge_total = edge_counts[member, round_index]
            src_row = edge_src[member, round_index]
            rel_row = edge_rel[member, round_index]
            dst_row = edge_dst[member, round_index]
            neg_rows = negatives[member, round_index]

            def batch_step(position, loop_state):
                src_grad, dst_grad, rel_acc = loop_state
                first_edge = position * BATCH
                src_ids = lax.dynamic_slice_in_dim(src_row, first_edge, BATCH)
                rel_ids = lax.dynamic_slice_in_dim(rel_row, first_edge, BATCH)
                dst_ids = lax.dynamic_slice_in_dim(dst_row, first_edge, BATCH)
                neg_ids = lax.dynamic_index_in_dim(neg_rows, position, 0, keepdims=False)
                live_edges = ((first_edge + jnp.arange(BATCH, dtype=jnp.int32)) < edge_total).astype(jnp.float32)
                grad_source, grad_relation, grad_target, grad_sampled = batch_terms(own_bf, mate_bf, rel_table, src_ids, rel_ids, dst_ids, neg_ids, live_edges)
                src_grad = src_grad.at[src_ids].add(grad_source)
                dst_grad = dst_grad.at[dst_ids].add(grad_target).at[neg_ids].add(grad_sampled)
                rel_acc = rel_acc.at[rel_ids].add(grad_relation)
                return (src_grad, dst_grad, rel_acc)

            batches_used = (edge_total + BATCH - 1) // BATCH
            zeros_block = jnp.zeros((ENT_DEV, D), jnp.float32)
            src_grad, dst_grad, rel_carry = lax.fori_loop(0, batches_used, batch_step, (zeros_block, zeros_block, rel_carry))
            return rel_carry, (src_grad, dst_grad)

        rel_grads, (src_grads, dst_grads) = lax.scan(per_partition, rel_grads, members)
        round_grad = src_grads + dst_grads[partner]
        grad_total = grad_total + round_grad
        blocks = blocks - step_size * round_grad
    return grad_total.reshape(ENTITIES, D), rel_grads
```

```python
import functools

import jax
import jax.numpy as jnp
from jax import lax
from jax.experimental import pallas as pl
from jax.experimental.pallas import tpu as pltpu
from jax.sharding import PartitionSpec as P

step_size = 0.1
LANES = 128
VMEM_LIMIT = 48 * 1024 * 1024
f32, bf16, i32 = jnp.float32, jnp.bfloat16, jnp.int32


def as_column(ids):
    return jnp.transpose(jnp.broadcast_to(ids, (LANES, ids.shape[1])))


def hot_columns(column, count):
    lane = lax.broadcasted_iota(i32, column.shape, 1)
    return jnp.concatenate(
        [jnp.where(column == lane + t, 1.0, 0.0) for t in range(0, count, LANES)], axis=1
    )


def hot_rows(ids, first, count):
    row = lax.broadcasted_iota(i32, (count, ids.shape[1]), 0) + first
    return jnp.where(row == ids, 1.0, 0.0).astype(bf16)


def dot(a, b):
    return jnp.dot(a, b, preferred_element_type=f32)


def pick_relations_kernel(rel_ref, ids_ref, out_ref, table_ref):
    r, c = pl.program_id(0), pl.program_id(1)
    rows = out_ref.shape[0]

    @pl.when((r == 0) & (c == 0))
    def _():
        table_ref[...] = rel_ref[...].astype(bf16)

    ids = ids_ref[0, pl.ds(r, 1), pl.ds(pl.multiple_of(c * rows, rows), rows)]
    hot = hot_columns(as_column(ids), table_ref.shape[0]).astype(bf16)
    out_ref[...] = dot(hot, table_ref[...]).astype(bf16)


def pick_relations(relations, edge_rel, rows):
    _, rounds, edges = edge_rel.shape
    rel, width = relations.shape
    steps = edges // rows
    return pl.pallas_call(
        pick_relations_kernel,
        grid=(rounds, steps),
        in_specs=[
            pl.BlockSpec((rel, width), lambda r, c: (0, 0)),
            pl.BlockSpec(edge_rel.shape, lambda r, c: (0, 0, 0)),
        ],
        out_specs=pl.BlockSpec((rows, width), lambda r, c: (r * steps + c, 0)),
        out_shape=jax.ShapeDtypeStruct((rounds * edges, width), bf16),
        scratch_shapes=[pltpu.VMEM((rel, width), bf16)],
        compiler_params=pltpu.CompilerParams(vmem_limit_bytes=VMEM_LIMIT),
        name="pick_relations",
    )(relations, edge_rel)


def spread_relations_kernel(ids_ref, dw0, dw1, dw2, dw3, out_ref):
    count = out_ref.shape[0]
    first = pl.program_id(0) * count
    total = None
    for r, dw in enumerate((dw0, dw1, dw2, dw3)):
        part = dot(hot_rows(ids_ref[0, r : r + 1, :], first, count), dw[...])
        total = part if total is None else total + part
    out_ref[...] = total


def spread_relations(edge_rel, dws, rel):
    width = dws[0].shape[1]
    tile = 384 if rel % 384 == 0 else 128
    return pl.pallas_call(
        spread_relations_kernel,
        grid=(rel // tile,),
        in_specs=[pl.BlockSpec(edge_rel.shape, lambda t: (0, 0, 0))]
        + [pl.BlockSpec(dw.shape, lambda t: (0, 0)) for dw in dws],
        out_specs=pl.BlockSpec((tile, width), lambda t: (t, 0)),
        out_shape=jax.ShapeDtypeStruct((rel, width), f32),
        compiler_params=pltpu.CompilerParams(vmem_limit_bytes=VMEM_LIMIT),
        name="spread_relations",
    )(edge_rel, *dws)


def round_kernel(
    r, count_ref, ent_ref, mate_ref, w_ref, src_ref, dst_ref, neg_ref, src_grad, dst_grad, dw_ref
):
    rows, width = ent_ref.shape
    half = width // 2
    edges = src_ref.shape[2]
    batches, negs = neg_ref.shape[2:]
    batch = edges // batches
    chunk = 2 * batch
    own = ent_ref[...].astype(bf16)
    mate = mate_ref[...]
    total = count_ref[0, r]
    ones = jnp.ones((8, negs), bf16)
    src_sum = dst_sum = None
    for c in range(edges // chunk):
        span = slice(c * chunk, (c + 1) * chunk)
        src_ids = src_ref[0, r : r + 1, span]
        dst_mask = hot_columns(as_column(dst_ref[0, r : r + 1, span]), rows)
        source = dot(hot_columns(as_column(src_ids), rows).astype(bf16), own)
        a_re, a_im = source[:, :half], source[:, half:]
        w = w_ref[span, :].astype(f32)
        w_re, w_im = w[:, :half], w[:, half:]
        u = jnp.concatenate(
            [a_re * w_re - a_im * w_im, a_re * w_im + a_im * w_re], axis=1
        ).astype(bf16)
        score = lax.dot_general(u, mate, (((1,), (1,)), ((), ())), preferred_element_type=f32)
        positive = jnp.sum(dst_mask * score, axis=1, keepdims=True)
        times = []
        for b in (2 * c, 2 * c + 1):
            hot = hot_rows(neg_ref[0, r, b : b + 1, :], 0, rows)
            seen = lax.dot_general(ones, hot, (((1,), (1,)), ((), ())), preferred_element_type=f32)
            times.append(jnp.broadcast_to(seen[:1], (batch, rows)))
        slot = lax.broadcasted_iota(i32, (chunk, rows), 0) + c * chunk
        times = jnp.where(slot < total, jnp.concatenate(times, axis=0) * (1.0 / negs), 0.0)
        weight = times * jax.nn.sigmoid(score - positive)
        pull = -jnp.sum(weight, axis=1, keepdims=True)
        weight = (weight + pull * dst_mask).astype(bf16)
        du = dot(weight, mate)
        part = lax.dot_general(weight, u, (((0,), (0,)), ((), ())), preferred_element_type=f32)
        dst_sum = part if dst_sum is None else dst_sum + part
        g_re, g_im = du[:, :half], du[:, half:]
        dw_ref[span, :] = jnp.concatenate(
            [g_re * a_re + g_im * a_im, g_im * a_re - g_re * a_im], axis=1
        ).astype(bf16)
        da = jnp.concatenate(
            [g_re * w_re + g_im * w_im, g_im * w_re - g_re * w_im], axis=1
        ).astype(bf16)
        part = dot(hot_rows(src_ids, 0, rows), da)
        src_sum = part if src_sum is None else src_sum + part
    src_grad[...] = src_sum
    dst_grad[...] = dst_sum.astype(bf16)


def run_round(r, edge_counts, entities, mate, w_all, edge_src, edge_dst, negatives):
    rows, width = entities.shape
    edges = edge_src.shape[2]
    whole = lambda x: pl.BlockSpec(x.shape, lambda i: (0,) * x.ndim)
    return pl.pallas_call(
        functools.partial(round_kernel, r),
        grid=(1,),
        in_specs=[
            pl.BlockSpec(memory_space=pltpu.SMEM),
            whole(entities),
            whole(mate),
            pl.BlockSpec((edges, width), lambda i: (r, 0)),
            whole(edge_src),
            whole(edge_dst),
            whole(negatives),
        ],
        out_specs=[
            pl.BlockSpec((rows, width), lambda i: (0, 0)),
            pl.BlockSpec((rows, width), lambda i: (0, 0)),
            pl.BlockSpec((edges, width), lambda i: (0, 0)),
        ],
        out_shape=[
            jax.ShapeDtypeStruct((rows, width), f32),
            jax.ShapeDtypeStruct((rows, width), bf16),
            jax.ShapeDtypeStruct((edges, width), bf16),
        ],
        compiler_params=pltpu.CompilerParams(vmem_limit_bytes=VMEM_LIMIT),
        name="train_round",
    )(edge_counts, entities, mate, w_all, edge_src, edge_dst, negatives)


def exchange(value, mask):
    size = lax.axis_size("dom")
    hops = [
        functools.partial(
            lax.ppermute, axis_name="dom", perm=[(i, i ^ m) for i in range(size)]
        )
        for m in range(1, size)
    ]
    return lax.switch(mask - 1, hops, value)


def local(entities, relations, edge_src, edge_rel, edge_dst, negatives, plan, edge_counts):
    edges = edge_src.shape[2]
    w_all = pick_relations(relations, edge_rel, 256)
    grad_total = jnp.zeros(entities.shape, f32)
    dws = []
    for r in range(plan.shape[0]):
        mate = exchange(entities.astype(bf16), plan[r])
        own_grad, mate_grad, dw = run_round(
            r, edge_counts, entities, mate, w_all, edge_src, edge_dst, negatives
        )
        dws.append(dw)
        grad = own_grad + exchange(mate_grad, plan[r]).astype(f32)
        grad_total = grad_total + grad
        entities = entities - step_size * grad
    rel_acc = spread_relations(edge_rel, dws, relations.shape[0])
    rel_shard = lax.psum_scatter(rel_acc, "dom", scatter_dimension=0, tiled=True)
    return grad_total, lax.psum(rel_shard, "grp")


def solution(mesh):
    both = ("grp", "dom")
    placed = (
        P(both, None),
        P(),
        P(both, None, None),
        P(both, None, None),
        P(both, None, None),
        P(both, None, None, None),
        P(),
        P(both, None),
    )
    return jax.shard_map(
        local,
        mesh=mesh,
        in_specs=placed,
        out_specs=(P(both, None), P("dom", None)),
        check_vma=False,
    )
```

```python
import functools

import jax
import jax.numpy as jnp
from jax import lax
from jax.experimental import pallas as pl
from jax.experimental.pallas import tpu as pltpu
from jax.sharding import PartitionSpec as P

step_size = 0.1
LANES = 128
VMEM_LIMIT = 48 * 1024 * 1024
MESH = pl.DeviceIdType.MESH
f32, bf16, i32 = jnp.float32, jnp.bfloat16, jnp.int32


def as_column(ids):
    return jnp.transpose(jnp.broadcast_to(ids, (LANES, ids.shape[1])))


def hot_columns(column, count):
    lane = lax.broadcasted_iota(i32, column.shape, 1)
    return jnp.concatenate(
        [jnp.where(column == lane + t, 1.0, 0.0) for t in range(0, count, LANES)], axis=1
    )


def hot_rows(ids, first, count):
    row = lax.broadcasted_iota(i32, (count, ids.shape[1]), 0) + first
    return jnp.where(row == ids, 1.0, 0.0).astype(bf16)


def dot(a, b):
    return jnp.dot(a, b, preferred_element_type=f32)


def pick_relations_kernel(rel_ref, ids_ref, out_ref, table_ref):
    r, c = pl.program_id(0), pl.program_id(1)
    rows = out_ref.shape[0]

    @pl.when((r == 0) & (c == 0))
    def _():
        table_ref[...] = rel_ref[...].astype(bf16)

    ids = ids_ref[0, pl.ds(r, 1), pl.ds(pl.multiple_of(c * rows, rows), rows)]
    hot = hot_columns(as_column(ids), table_ref.shape[0]).astype(bf16)
    out_ref[...] = dot(hot, table_ref[...]).astype(bf16)


def pick_relations(relations, edge_rel, rows):
    _, rounds, edges = edge_rel.shape
    rel, width = relations.shape
    steps = edges // rows
    return pl.pallas_call(
        pick_relations_kernel,
        grid=(rounds, steps),
        in_specs=[
            pl.BlockSpec((rel, width), lambda r, c: (0, 0)),
            pl.BlockSpec(edge_rel.shape, lambda r, c: (0, 0, 0)),
        ],
        out_specs=pl.BlockSpec((rows, width), lambda r, c: (r * steps + c, 0)),
        out_shape=jax.ShapeDtypeStruct((rounds * edges, width), bf16),
        scratch_shapes=[pltpu.VMEM((rel, width), bf16)],
        compiler_params=pltpu.CompilerParams(vmem_limit_bytes=VMEM_LIMIT),
        name="pick_relations",
    )(relations, edge_rel)


def reduce_relations_kernel(
    groups,
    size,
    stride,
    ids_ref,
    dw0,
    dw1,
    dw2,
    dw3,
    out_ref,
    own_sum,
    core_out,
    core_in,
    group_out,
    group_in,
    chip_out,
    chip_in,
    share_out,
    share_in,
    core_sems,
    group_sems,
    chip_sems,
    share_sems,
):
    g, d = lax.axis_index("grp"), lax.axis_index("dom")
    core, chip = lax.rem(d, 2), lax.div(d, 2)
    chips = size // 2
    pad = own_sum.shape[1]
    rows = pad // groups

    def flip(index, mask):
        bits = [lax.rem(lax.div(index, 1 << b), 2) for b in range(mask.bit_length())]
        return index + sum(
            ((1 - 2 * bit) << b for b, bit in enumerate(bits) if mask >> b & 1), jnp.int32(0)
        )

    mate = flip(d, 1)
    group_mates = [flip(g, k) for k in range(1, groups)]
    chip_mates = [flip(chip, k) for k in range(1, chips)]
    greet = [(g, mate)] + [(m, d) for m in group_mates] + [(g, 2 * m + core) for m in chip_mates]
    barrier = pltpu.get_barrier_semaphore()
    for device in greet:
        pl.semaphore_signal(barrier, inc=1, device_id=device, device_id_type=MESH)
    pl.semaphore_wait(barrier, len(greet))

    def send(source, target, sems, at, device):
        return pltpu.make_async_remote_copy(
            src_ref=source,
            dst_ref=target,
            send_sem=sems.at[(0,) + at],
            recv_sem=sems.at[(1,) + at],
            device_id=device,
            device_id_type=MESH,
        )

    def partial_sum(index):
        total = None
        for r, dw in enumerate((dw0, dw1, dw2, dw3)):
            part = dot(hot_rows(ids_ref[0, r : r + 1, :], index * stride, pad), dw[...])
            total = part if total is None else total + part
        return total

    def to_core(i):
        return send(core_out.at[i], core_in.at[i], core_sems, (i,), (g, mate))

    def to_group(i, k):
        m = group_mates[k]
        there = pl.ds(pl.multiple_of(m * rows, rows), rows)
        return send(
            group_out.at[i, there], group_in.at[k, i], group_sems, (k, i), (m, d)
        )

    def first(i, carry):
        core_out[i] = partial_sum(2 * i + 1 - core).astype(bf16)
        to_core(i).start()
        return carry

    lax.fori_loop(0, chips, first, 0)

    def second(i, carry):
        own = partial_sum(2 * i + core)
        to_core(i).wait()
        own = own + core_in[i].astype(f32)
        own_sum[i] = own
        group_out[i] = own.astype(bf16)
        for k in range(groups - 1):
            to_group(i, k).start()
        return carry

    lax.fori_loop(0, chips, second, 0)
    here = pl.ds(pl.multiple_of(g * rows, rows), rows)

    def third(i, carry):
        total = own_sum[i, here]
        for k in range(groups - 1):
            to_group(i, k).wait()
            total = total + group_in[k, i].astype(f32)
        own_sum[i, here] = total
        chip_out[i] = total.astype(bf16)
        return carry

    lax.fori_loop(0, chips, third, 0)
    copies = [
        send(chip_out.at[m], chip_in.at[k], chip_sems, (k,), (g, 2 * m + core))
        for k, m in enumerate(chip_mates)
    ]
    for copy in copies:
        copy.start()
    total = own_sum[chip, here]
    for k, copy in enumerate(copies):
        copy.wait()
        total = total + chip_in[k].astype(f32)
    share_out[...] = total.astype(bf16)
    copies = [
        send(share_out, share_in.at[k], share_sems, (k,), (m, d))
        for k, m in enumerate(group_mates)
    ]
    for copy in copies:
        copy.start()
    out_ref[here, :] = share_out[...].astype(f32)
    for k, (copy, m) in enumerate(zip(copies, group_mates)):
        copy.wait()
        out_ref[pl.ds(pl.multiple_of(m * rows, rows), rows), :] = share_in[k].astype(f32)


def reduce_relations(edge_rel, dws, rel):
    width = dws[0].shape[1]
    groups, size = lax.axis_size("grp"), lax.axis_size("dom")
    chips = size // 2
    stride = rel // size
    rows = -(-stride // (16 * groups)) * 16
    pad = rows * groups
    whole = pl.BlockSpec(memory_space=pltpu.VMEM)
    dma = lambda *shape: pltpu.SemaphoreType.DMA((2,) + shape)
    out = pl.pallas_call(
        functools.partial(reduce_relations_kernel, groups, size, stride),
        in_specs=[whole] * (1 + len(dws)),
        out_specs=whole,
        out_shape=jax.ShapeDtypeStruct((pad, width), f32),
        scratch_shapes=[
            pltpu.VMEM((chips, pad, width), f32),
            pltpu.VMEM((chips, pad, width), bf16),
            pltpu.VMEM((chips, pad, width), bf16),
            pltpu.VMEM((chips, pad, width), bf16),
            pltpu.VMEM((groups - 1, chips, rows, width), bf16),
            pltpu.VMEM((chips, rows, width), bf16),
            pltpu.VMEM((chips - 1, rows, width), bf16),
            pltpu.VMEM((rows, width), bf16),
            pltpu.VMEM((groups - 1, rows, width), bf16),
            dma(chips),
            dma(groups - 1, chips),
            dma(chips - 1),
            dma(groups - 1),
        ],
        compiler_params=pltpu.CompilerParams(
            vmem_limit_bytes=VMEM_LIMIT, collective_id=0, has_side_effects=True
        ),
        name="reduce_relations",
    )(edge_rel, *dws)
    return out[:stride]


def round_kernel(
    r, count_ref, ent_ref, mate_ref, w_ref, src_ref, dst_ref, neg_ref, src_grad, dst_grad, dw_ref
):
    rows, width = ent_ref.shape
    half = width // 2
    edges = src_ref.shape[2]
    batches, negs = neg_ref.shape[2:]
    batch = edges // batches
    chunk = 2 * batch
    own = ent_ref[...].astype(bf16)
    mate = mate_ref[...]
    total = count_ref[0, r]
    ones = jnp.ones((8, negs), bf16)
    src_sum = dst_sum = None
    for c in range(edges // chunk):
        span = slice(c * chunk, (c + 1) * chunk)
        src_ids = src_ref[0, r : r + 1, span]
        dst_mask = hot_columns(as_column(dst_ref[0, r : r + 1, span]), rows)
        source = dot(hot_columns(as_column(src_ids), rows).astype(bf16), own)
        a_re, a_im = source[:, :half], source[:, half:]
        w = w_ref[span, :].astype(f32)
        w_re, w_im = w[:, :half], w[:, half:]
        u = jnp.concatenate(
            [a_re * w_re - a_im * w_im, a_re * w_im + a_im * w_re], axis=1
        ).astype(bf16)
        score = lax.dot_general(u, mate, (((1,), (1,)), ((), ())), preferred_element_type=f32)
        positive = jnp.sum(dst_mask * score, axis=1, keepdims=True)
        times = []
        for b in (2 * c, 2 * c + 1):
            hot = hot_rows(neg_ref[0, r, b : b + 1, :], 0, rows)
            seen = lax.dot_general(ones, hot, (((1,), (1,)), ((), ())), preferred_element_type=f32)
            times.append(jnp.broadcast_to(seen[:1], (batch, rows)))
        slot = lax.broadcasted_iota(i32, (chunk, rows), 0) + c * chunk
        times = jnp.where(slot < total, jnp.concatenate(times, axis=0) * (1.0 / negs), 0.0)
        weight = times * jax.nn.sigmoid(score - positive)
        pull = -jnp.sum(weight, axis=1, keepdims=True)
        weight = (weight + pull * dst_mask).astype(bf16)
        du = dot(weight, mate)
        part = lax.dot_general(weight, u, (((0,), (0,)), ((), ())), preferred_element_type=f32)
        dst_sum = part if dst_sum is None else dst_sum + part
        g_re, g_im = du[:, :half], du[:, half:]
        dw_ref[span, :] = jnp.concatenate(
            [g_re * a_re + g_im * a_im, g_im * a_re - g_re * a_im], axis=1
        ).astype(bf16)
        da = jnp.concatenate(
            [g_re * w_re + g_im * w_im, g_im * w_re - g_re * w_im], axis=1
        ).astype(bf16)
        part = dot(hot_rows(src_ids, 0, rows), da)
        src_sum = part if src_sum is None else src_sum + part
    src_grad[...] = src_sum
    dst_grad[...] = dst_sum.astype(bf16)


def run_round(r, edge_counts, entities, mate, w_all, edge_src, edge_dst, negatives):
    rows, width = entities.shape
    edges = edge_src.shape[2]
    whole = lambda x: pl.BlockSpec(x.shape, lambda i: (0,) * x.ndim)
    return pl.pallas_call(
        functools.partial(round_kernel, r),
        grid=(1,),
        in_specs=[
            pl.BlockSpec(memory_space=pltpu.SMEM),
            whole(entities),
            whole(mate),
            pl.BlockSpec((edges, width), lambda i: (r, 0)),
            whole(edge_src),
            whole(edge_dst),
            whole(negatives),
        ],
        out_specs=[
            pl.BlockSpec((rows, width), lambda i: (0, 0)),
            pl.BlockSpec((rows, width), lambda i: (0, 0)),
            pl.BlockSpec((edges, width), lambda i: (0, 0)),
        ],
        out_shape=[
            jax.ShapeDtypeStruct((rows, width), f32),
            jax.ShapeDtypeStruct((rows, width), bf16),
            jax.ShapeDtypeStruct((edges, width), bf16),
        ],
        compiler_params=pltpu.CompilerParams(vmem_limit_bytes=VMEM_LIMIT),
        name="train_round",
    )(edge_counts, entities, mate, w_all, edge_src, edge_dst, negatives)


def exchange(value, mask):
    size = lax.axis_size("dom")
    hops = [
        functools.partial(
            lax.ppermute, axis_name="dom", perm=[(i, i ^ m) for i in range(size)]
        )
        for m in range(1, size)
    ]
    return lax.switch(mask - 1, hops, value)


def local(entities, relations, edge_src, edge_rel, edge_dst, negatives, plan, edge_counts):
    edges = edge_src.shape[2]
    w_all = pick_relations(relations, edge_rel, 256)
    grad_total = jnp.zeros(entities.shape, f32)
    dws = []
    for r in range(plan.shape[0]):
        mate = exchange(entities.astype(bf16), plan[r])
        own_grad, mate_grad, dw = run_round(
            r, edge_counts, entities, mate, w_all, edge_src, edge_dst, negatives
        )
        dws.append(dw)
        grad = own_grad + exchange(mate_grad, plan[r]).astype(f32)
        grad_total = grad_total + grad
        entities = entities - step_size * grad
    return grad_total, reduce_relations(edge_rel, dws, relations.shape[0])


def solution(mesh):
    both = ("grp", "dom")
    placed = (
        P(both, None),
        P(),
        P(both, None, None),
        P(both, None, None),
        P(both, None, None),
        P(both, None, None, None),
        P(),
        P(both, None),
    )
    return jax.shard_map(
        local,
        mesh=mesh,
        in_specs=placed,
        out_specs=(P(both, None), P("dom", None)),
        check_vma=False,
    )
```

```python
import functools

import jax
import jax.numpy as jnp
from jax import lax
from jax.experimental import pallas as pl
from jax.experimental.pallas import tpu as pltpu
from jax.sharding import PartitionSpec as P

step_size = 0.1
LANES = 128
VMEM_LIMIT = 48 * 1024 * 1024
MESH = pl.DeviceIdType.MESH
f32, bf16, i32 = jnp.float32, jnp.bfloat16, jnp.int32


def as_column(ids):
    return jnp.transpose(jnp.broadcast_to(ids, (LANES, ids.shape[1])))


def hot_columns(column, count):
    lane = lax.broadcasted_iota(i32, column.shape, 1)
    return jnp.concatenate(
        [jnp.where(column == lane + t, 1.0, 0.0) for t in range(0, count, LANES)], axis=1
    )


def hot_rows(ids, first, count):
    row = lax.broadcasted_iota(i32, (count, ids.shape[1]), 0) + first
    return jnp.where(row == ids, 1.0, 0.0).astype(bf16)


def dot(a, b):
    return jnp.dot(a, b, preferred_element_type=f32)


def pick_relations_kernel(r, rel_ref, ids_ref, out_ref, table_ref=None):
    c = pl.program_id(0)
    rows = out_ref.shape[0]
    if table_ref is not None:

        @pl.when(c == 0)
        def _():
            table_ref[...] = rel_ref[...].astype(bf16)

        rel_ref = table_ref

    ids = ids_ref[0, r : r + 1, pl.ds(pl.multiple_of(c * rows, rows), rows)]
    hot = hot_columns(as_column(ids), rel_ref.shape[0]).astype(bf16)
    out_ref[...] = dot(hot, rel_ref[...]).astype(bf16)


def pick_relations(relations, edge_rel, r, rows):
    edges = edge_rel.shape[2]
    rel, width = relations.shape
    table = pl.BlockSpec((rel, width), lambda c: (0, 0))
    wide = relations.dtype != bf16
    out = pl.pallas_call(
        functools.partial(pick_relations_kernel, r),
        grid=(edges // rows,),
        in_specs=[table, pl.BlockSpec(edge_rel.shape, lambda c: (0, 0, 0))],
        out_specs=[pl.BlockSpec((rows, width), lambda c: (c, 0))] + [table] * wide,
        out_shape=[jax.ShapeDtypeStruct((edges, width), bf16)]
        + [jax.ShapeDtypeStruct((rel, width), bf16)] * wide,
        compiler_params=pltpu.CompilerParams(vmem_limit_bytes=VMEM_LIMIT),
        cost_estimate=pl.CostEstimate(
            flops=2 * edges * rel * width, bytes_accessed=2 * (rel + edges) * width, transcendentals=0
        ),
        name="pick_relations",
    )(relations, edge_rel)
    return out if wide else out[0]


def reduce_relations_kernel(
    groups,
    size,
    stride,
    ids_ref,
    dw0,
    dw1,
    dw2,
    dw3,
    out_ref,
    own_sum,
    core_out,
    core_in,
    group_out,
    group_in,
    chip_out,
    chip_in,
    share_out,
    share_in,
    core_sems,
    group_sems,
    chip_sems,
    share_sems,
):
    g, d = lax.axis_index("grp"), lax.axis_index("dom")
    core, chip = lax.rem(d, 2), lax.div(d, 2)
    chips = size // 2
    pad = own_sum.shape[1]
    rows = pad // groups

    def flip(index, mask):
        bits = [lax.rem(lax.div(index, 1 << b), 2) for b in range(mask.bit_length())]
        return index + sum(
            ((1 - 2 * bit) << b for b, bit in enumerate(bits) if mask >> b & 1), jnp.int32(0)
        )

    mate = flip(d, 1)
    group_mates = [flip(g, k) for k in range(1, groups)]
    chip_mates = [flip(chip, k) for k in range(1, chips)]
    greet = [(g, mate)] + [(m, d) for m in group_mates] + [(g, 2 * m + core) for m in chip_mates]
    barrier = pltpu.get_barrier_semaphore()
    for device in greet:
        pl.semaphore_signal(barrier, inc=1, device_id=device, device_id_type=MESH)
    pl.semaphore_wait(barrier, len(greet))

    def send(source, target, sems, at, device):
        return pltpu.make_async_remote_copy(
            src_ref=source,
            dst_ref=target,
            send_sem=sems.at[(0,) + at],
            recv_sem=sems.at[(1,) + at],
            device_id=device,
            device_id_type=MESH,
        )

    def partial_sum(index):
        total = None
        for r, dw in enumerate((dw0, dw1, dw2, dw3)):
            part = dot(hot_rows(ids_ref[0, r : r + 1, :], index * stride, pad), dw[...])
            total = part if total is None else total + part
        return total

    def to_core(i):
        return send(core_out.at[i], core_in.at[i], core_sems, (i,), (g, mate))

    def to_group(i, k):
        m = group_mates[k]
        there = pl.ds(pl.multiple_of(m * rows, rows), rows)
        return send(
            group_out.at[i, there], group_in.at[k, i], group_sems, (k, i), (m, d)
        )

    def first(i, carry):
        core_out[i] = partial_sum(2 * i + 1 - core)
        to_core(i).start()
        return carry

    lax.fori_loop(0, chips, first, 0)

    def second(i, carry):
        own = partial_sum(2 * i + core)
        to_core(i).wait()
        own = own + core_in[i]
        own_sum[i] = own
        group_out[i] = own.astype(bf16)
        for k in range(groups - 1):
            to_group(i, k).start()
        return carry

    lax.fori_loop(0, chips, second, 0)
    here = pl.ds(pl.multiple_of(g * rows, rows), rows)

    def third(i, carry):
        total = own_sum[i, here]
        for k in range(groups - 1):
            to_group(i, k).wait()
            total = total + group_in[k, i].astype(f32)
        own_sum[i, here] = total
        chip_out[i] = total.astype(bf16)
        return carry

    lax.fori_loop(0, chips, third, 0)
    copies = [
        send(chip_out.at[m], chip_in.at[k], chip_sems, (k,), (g, 2 * m + core))
        for k, m in enumerate(chip_mates)
    ]
    for copy in copies:
        copy.start()
    total = own_sum[chip, here]
    for k, copy in enumerate(copies):
        copy.wait()
        total = total + chip_in[k].astype(f32)
    share_out[...] = total
    copies = [
        send(share_out, share_in.at[k], share_sems, (k,), (m, d))
        for k, m in enumerate(group_mates)
    ]
    for copy in copies:
        copy.start()
    out_ref[here, :] = share_out[...]
    for k, (copy, m) in enumerate(zip(copies, group_mates)):
        copy.wait()
        out_ref[pl.ds(pl.multiple_of(m * rows, rows), rows), :] = share_in[k]


def reduce_relations(edge_rel, dws, rel):
    width = dws[0].shape[1]
    groups, size = lax.axis_size("grp"), lax.axis_size("dom")
    chips = size // 2
    stride = rel // size
    rows = -(-stride // (16 * groups)) * 16
    pad = rows * groups
    whole = pl.BlockSpec(memory_space=pltpu.VMEM)
    dma = lambda *shape: pltpu.SemaphoreType.DMA((2,) + shape)
    out = pl.pallas_call(
        functools.partial(reduce_relations_kernel, groups, size, stride),
        in_specs=[whole] * (1 + len(dws)),
        out_specs=whole,
        out_shape=jax.ShapeDtypeStruct((pad, width), f32),
        scratch_shapes=[
            pltpu.VMEM((chips, pad, width), f32),
            pltpu.VMEM((chips, pad, width), f32),
            pltpu.VMEM((chips, pad, width), f32),
            pltpu.VMEM((chips, pad, width), bf16),
            pltpu.VMEM((groups - 1, chips, rows, width), bf16),
            pltpu.VMEM((chips, rows, width), bf16),
            pltpu.VMEM((chips - 1, rows, width), bf16),
            pltpu.VMEM((rows, width), f32),
            pltpu.VMEM((groups - 1, rows, width), f32),
            dma(chips),
            dma(groups - 1, chips),
            dma(chips - 1),
            dma(groups - 1),
        ],
        compiler_params=pltpu.CompilerParams(
            vmem_limit_bytes=VMEM_LIMIT, collective_id=0, has_side_effects=True
        ),
        name="reduce_relations",
    )(edge_rel, *dws)
    return out[:stride]


def round_kernel(
    r, count_ref, ent_ref, mate_ref, w_ref, src_ref, dst_ref, neg_ref, src_grad, dst_grad, dw_ref
):
    rows, width = ent_ref.shape
    half = width // 2
    edges = src_ref.shape[2]
    batches, negs = neg_ref.shape[2:]
    batch = edges // batches
    chunk = 2 * batch
    own = ent_ref[...].astype(bf16)
    mate = mate_ref[...]
    total = count_ref[0, r]
    ones = jnp.ones((8, negs), bf16)
    src_sum = dst_sum = None
    for c in range(edges // chunk):
        span = slice(c * chunk, (c + 1) * chunk)
        src_ids = src_ref[0, r : r + 1, span]
        dst_mask = hot_columns(as_column(dst_ref[0, r : r + 1, span]), rows)
        source = dot(hot_columns(as_column(src_ids), rows).astype(bf16), own)
        a_re, a_im = source[:, :half], source[:, half:]
        w = w_ref[span, :].astype(f32)
        w_re, w_im = w[:, :half], w[:, half:]
        u = jnp.concatenate(
            [a_re * w_re - a_im * w_im, a_re * w_im + a_im * w_re], axis=1
        ).astype(bf16)
        score = lax.dot_general(u, mate, (((1,), (1,)), ((), ())), preferred_element_type=f32)
        positive = jnp.sum(dst_mask * score, axis=1, keepdims=True)
        times = []
        for b in (2 * c, 2 * c + 1):
            hot = hot_rows(neg_ref[0, r, b : b + 1, :], 0, rows)
            seen = lax.dot_general(ones, hot, (((1,), (1,)), ((), ())), preferred_element_type=f32)
            times.append(jnp.broadcast_to(seen[:1], (batch, rows)))
        slot = lax.broadcasted_iota(i32, (chunk, rows), 0) + c * chunk
        times = jnp.where(slot < total, jnp.concatenate(times, axis=0) * (1.0 / negs), 0.0)
        weight = times * jax.nn.sigmoid(score - positive)
        pull = -jnp.sum(weight, axis=1, keepdims=True)
        weight = (weight + pull * dst_mask).astype(bf16)
        du = dot(weight, mate)
        part = lax.dot_general(weight, u, (((0,), (0,)), ((), ())), preferred_element_type=f32)
        dst_sum = part if dst_sum is None else dst_sum + part
        g_re, g_im = du[:, :half], du[:, half:]
        dw_ref[span, :] = jnp.concatenate(
            [g_re * a_re + g_im * a_im, g_im * a_re - g_re * a_im], axis=1
        ).astype(bf16)
        da = jnp.concatenate(
            [g_re * w_re + g_im * w_im, g_im * w_re - g_re * w_im], axis=1
        ).astype(bf16)
        part = dot(hot_rows(src_ids, 0, rows), da)
        src_sum = part if src_sum is None else src_sum + part
    src_grad[...] = src_sum
    dst_grad[...] = dst_sum.astype(bf16)


def run_round(r, edge_counts, entities, mate, w, edge_src, edge_dst, negatives):
    rows, width = entities.shape
    edges = edge_src.shape[2]
    whole = lambda x: pl.BlockSpec(x.shape, lambda i: (0,) * x.ndim)
    return pl.pallas_call(
        functools.partial(round_kernel, r),
        grid=(1,),
        in_specs=[
            pl.BlockSpec(memory_space=pltpu.SMEM),
            whole(entities),
            whole(mate),
            whole(w),
            whole(edge_src),
            whole(edge_dst),
            whole(negatives),
        ],
        out_specs=[
            pl.BlockSpec((rows, width), lambda i: (0, 0)),
            pl.BlockSpec((rows, width), lambda i: (0, 0)),
            pl.BlockSpec((edges, width), lambda i: (0, 0)),
        ],
        out_shape=[
            jax.ShapeDtypeStruct((rows, width), f32),
            jax.ShapeDtypeStruct((rows, width), bf16),
            jax.ShapeDtypeStruct((edges, width), bf16),
        ],
        compiler_params=pltpu.CompilerParams(vmem_limit_bytes=VMEM_LIMIT),
        name="train_round",
    )(edge_counts, entities, mate, w, edge_src, edge_dst, negatives)


def exchange(value, mask, beside=None, *operands):
    size = lax.axis_size("dom")

    def hop(m, value, *operands):
        came = lax.ppermute(value, "dom", [(i, i ^ m) for i in range(size)])
        return came if beside is None else (came, beside(*operands))

    hops = [functools.partial(hop, m) for m in range(1, size)]
    return lax.switch(mask - 1, hops, value, *operands)


def local(entities, relations, edge_src, edge_rel, edge_dst, negatives, plan, edge_counts):
    grad_total = jnp.zeros(entities.shape, f32)
    w, table = pick_relations(relations, edge_rel, 0, 256)
    dws = []
    rounds = plan.shape[0]
    for r in range(rounds):
        mate = exchange(entities.astype(bf16), plan[r])
        own_grad, mate_grad, dw = run_round(
            r, edge_counts, entities, mate, w, edge_src, edge_dst, negatives
        )
        dws.append(dw)
        if r + 1 < rounds:
            pick = functools.partial(pick_relations, r=r + 1, rows=256)
            back, w = exchange(mate_grad, plan[r], pick, table, edge_rel)
        else:
            back = exchange(mate_grad, plan[r])
        grad = own_grad + back.astype(f32)
        grad_total = grad_total + grad
        entities = entities - step_size * grad
    return grad_total, reduce_relations(edge_rel, dws, relations.shape[0])


def solution(mesh):
    both = ("grp", "dom")
    placed = (
        P(both, None),
        P(),
        P(both, None, None),
        P(both, None, None),
        P(both, None, None),
        P(both, None, None, None),
        P(),
        P(both, None),
    )
    return jax.shard_map(
        local,
        mesh=mesh,
        in_specs=placed,
        out_specs=(P(both, None), P("dom", None)),
        check_vma=False,
    )
```

```python
import functools

import jax
import jax.numpy as jnp
from jax import lax
from jax.experimental import pallas as pl
from jax.experimental.pallas import tpu as pltpu
from jax.sharding import PartitionSpec as P

step_size = 0.1
LANES = 128
VMEM_LIMIT = 48 * 1024 * 1024
MESH = pl.DeviceIdType.MESH
f32, bf16, i32 = jnp.float32, jnp.bfloat16, jnp.int32


def as_column(ids):
    return jnp.transpose(jnp.broadcast_to(ids, (LANES, ids.shape[1])))


def hot_columns(column, count):
    lane = lax.broadcasted_iota(i32, column.shape, 1)
    return jnp.concatenate(
        [jnp.where(column == lane + t, 1.0, 0.0) for t in range(0, count, LANES)], axis=1
    )


def hot_rows(ids, first, count):
    row = lax.broadcasted_iota(i32, (count, ids.shape[1]), 0) + first
    return jnp.where(row == ids, 1.0, 0.0).astype(bf16)


def dot(a, b):
    return jnp.dot(a, b, preferred_element_type=f32)


def pick_relations_kernel(r, rel_ref, ids_ref, out_ref, table_ref=None):
    c = pl.program_id(0)
    rows = out_ref.shape[0]
    if table_ref is not None:

        @pl.when(c == 0)
        def _():
            table_ref[...] = rel_ref[...].astype(bf16)

        rel_ref = table_ref

    ids = ids_ref[0, r : r + 1, pl.ds(pl.multiple_of(c * rows, rows), rows)]
    hot = hot_columns(as_column(ids), rel_ref.shape[0]).astype(bf16)
    out_ref[...] = dot(hot, rel_ref[...]).astype(bf16)


def pick_relations(relations, edge_rel, r, rows):
    edges = edge_rel.shape[2]
    rel, width = relations.shape
    table = pl.BlockSpec((rel, width), lambda c: (0, 0))
    wide = relations.dtype != bf16
    out = pl.pallas_call(
        functools.partial(pick_relations_kernel, r),
        grid=(edges // rows,),
        in_specs=[table, pl.BlockSpec(edge_rel.shape, lambda c: (0, 0, 0))],
        out_specs=[pl.BlockSpec((rows, width), lambda c: (c, 0))] + [table] * wide,
        out_shape=[jax.ShapeDtypeStruct((edges, width), bf16)]
        + [jax.ShapeDtypeStruct((rel, width), bf16)] * wide,
        compiler_params=pltpu.CompilerParams(vmem_limit_bytes=VMEM_LIMIT),
        cost_estimate=pl.CostEstimate(
            flops=2 * edges * rel * width, bytes_accessed=2 * (rel + edges) * width, transcendentals=0
        ),
        name="pick_relations",
    )(relations, edge_rel)
    return out if wide else out[0]


def reduce_relations_kernel(
    groups,
    size,
    stride,
    ids_ref,
    dw0,
    dw1,
    dw2,
    dw3,
    out_ref,
    own_sum,
    core_out,
    core_in,
    group_out,
    group_in,
    chip_out,
    chip_in,
    share_out,
    share_in,
    core_sems,
    group_sems,
    chip_sems,
    share_sems,
):
    g, d = lax.axis_index("grp"), lax.axis_index("dom")
    core, chip = lax.rem(d, 2), lax.div(d, 2)
    chips = size // 2
    pad = own_sum.shape[1]
    rows = pad // groups

    def flip(index, mask):
        bits = [lax.rem(lax.div(index, 1 << b), 2) for b in range(mask.bit_length())]
        return index + sum(
            ((1 - 2 * bit) << b for b, bit in enumerate(bits) if mask >> b & 1), jnp.int32(0)
        )

    mate = flip(d, 1)
    group_mates = [flip(g, k) for k in range(1, groups)]
    chip_mates = [flip(chip, k) for k in range(1, chips)]
    greet = [(g, mate)] + [(m, d) for m in group_mates] + [(g, 2 * m + core) for m in chip_mates]
    barrier = pltpu.get_barrier_semaphore()
    for device in greet:
        pl.semaphore_signal(barrier, inc=1, device_id=device, device_id_type=MESH)
    pl.semaphore_wait(barrier, len(greet))

    def send(source, target, sems, at, device):
        return pltpu.make_async_remote_copy(
            src_ref=source,
            dst_ref=target,
            send_sem=sems.at[(0,) + at],
            recv_sem=sems.at[(1,) + at],
            device_id=device,
            device_id_type=MESH,
        )

    def partial_sum(index):
        total = None
        for r, dw in enumerate((dw0, dw1, dw2, dw3)):
            part = dot(hot_rows(ids_ref[0, r : r + 1, :], index * stride, pad), dw[...])
            total = part if total is None else total + part
        return total

    def to_core(i):
        return send(core_out.at[i], core_in.at[i], core_sems, (i,), (g, mate))

    def to_group(i, k):
        m = group_mates[k]
        there = pl.ds(pl.multiple_of(m * rows, rows), rows)
        return send(
            group_out.at[i, there], group_in.at[k, i], group_sems, (k, i), (m, d)
        )

    def first(i, carry):
        core_out[i] = partial_sum(2 * i + 1 - core)
        to_core(i).start()
        return carry

    lax.fori_loop(0, chips, first, 0)

    def second(i, carry):
        own = partial_sum(2 * i + core)
        to_core(i).wait()
        own = own + core_in[i]
        own_sum[i] = own
        group_out[i] = own.astype(bf16)
        for k in range(groups - 1):
            to_group(i, k).start()
        return carry

    lax.fori_loop(0, chips, second, 0)
    here = pl.ds(pl.multiple_of(g * rows, rows), rows)

    def third(i, carry):
        total = own_sum[i, here]
        for k in range(groups - 1):
            to_group(i, k).wait()
            total = total + group_in[k, i].astype(f32)
        own_sum[i, here] = total
        chip_out[i] = total.astype(bf16)
        return carry

    lax.fori_loop(0, chips, third, 0)
    copies = [
        send(chip_out.at[m], chip_in.at[k], chip_sems, (k,), (g, 2 * m + core))
        for k, m in enumerate(chip_mates)
    ]
    for copy in copies:
        copy.start()
    total = own_sum[chip, here]
    for k, copy in enumerate(copies):
        copy.wait()
        total = total + chip_in[k].astype(f32)
    share_out[...] = total
    copies = [
        send(share_out, share_in.at[k], share_sems, (k,), (m, d))
        for k, m in enumerate(group_mates)
    ]
    for copy in copies:
        copy.start()
    out_ref[here, :] = share_out[...]
    for k, (copy, m) in enumerate(zip(copies, group_mates)):
        copy.wait()
        out_ref[pl.ds(pl.multiple_of(m * rows, rows), rows), :] = share_in[k]


def reduce_relations(edge_rel, dws, rel):
    width = dws[0].shape[1]
    groups, size = lax.axis_size("grp"), lax.axis_size("dom")
    chips = size // 2
    stride = rel // size
    rows = -(-stride // (16 * groups)) * 16
    pad = rows * groups
    whole = pl.BlockSpec(memory_space=pltpu.VMEM)
    dma = lambda *shape: pltpu.SemaphoreType.DMA((2,) + shape)
    out = pl.pallas_call(
        functools.partial(reduce_relations_kernel, groups, size, stride),
        in_specs=[whole] * (1 + len(dws)),
        out_specs=whole,
        out_shape=jax.ShapeDtypeStruct((pad, width), f32),
        scratch_shapes=[
            pltpu.VMEM((chips, pad, width), f32),
            pltpu.VMEM((chips, pad, width), f32),
            pltpu.VMEM((chips, pad, width), f32),
            pltpu.VMEM((chips, pad, width), bf16),
            pltpu.VMEM((groups - 1, chips, rows, width), bf16),
            pltpu.VMEM((chips, rows, width), bf16),
            pltpu.VMEM((chips - 1, rows, width), bf16),
            pltpu.VMEM((rows, width), f32),
            pltpu.VMEM((groups - 1, rows, width), f32),
            dma(chips),
            dma(groups - 1, chips),
            dma(chips - 1),
            dma(groups - 1),
        ],
        compiler_params=pltpu.CompilerParams(
            vmem_limit_bytes=VMEM_LIMIT, collective_id=0, has_side_effects=True
        ),
        name="reduce_relations",
    )(edge_rel, *dws)
    return out[:stride]


def prepare_kernel(r, ent_ref, w_ref, src_ref, neg_ref, source_ref, product_ref, seen_ref):
    rows, width = ent_ref.shape
    half = width // 2
    batches, negs = neg_ref.shape[2:]
    edges = src_ref.shape[2]
    chunk = 2 * (edges // batches)
    own = ent_ref[...]
    ones = jnp.ones((8, negs), bf16)
    for c in range(edges // chunk):
        span = slice(c * chunk, (c + 1) * chunk)
        source = dot(hot_columns(as_column(src_ref[0, r : r + 1, span]), rows).astype(bf16), own)
        source_ref[span, :] = source.astype(bf16)
        a_re, a_im = source[:, :half], source[:, half:]
        w = w_ref[span, :].astype(f32)
        w_re, w_im = w[:, :half], w[:, half:]
        product_ref[span, :] = jnp.concatenate(
            [a_re * w_re - a_im * w_im, a_re * w_im + a_im * w_re], axis=1
        ).astype(bf16)
    for b in range(batches):
        hot = hot_rows(neg_ref[0, r, b : b + 1, :], 0, rows)
        seen = lax.dot_general(ones, hot, (((1,), (1,)), ((), ())), preferred_element_type=f32)
        seen_ref[b : b + 1, :] = seen[:1] * (1.0 / negs)


def whole(x):
    return pl.BlockSpec(x.shape, lambda i: (0,) * len(x.shape))


def prepare(own, w, edge_src, negatives, r):
    rows, width = own.shape
    edges, batches = edge_src.shape[2], negatives.shape[2]
    out = [
        jax.ShapeDtypeStruct((edges, width), bf16),
        jax.ShapeDtypeStruct((edges, width), bf16),
        jax.ShapeDtypeStruct((batches, rows), f32),
    ]
    return pl.pallas_call(
        functools.partial(prepare_kernel, r),
        grid=(1,),
        in_specs=[whole(x) for x in (own, w, edge_src, negatives)],
        out_specs=[whole(x) for x in out],
        out_shape=out,
        compiler_params=pltpu.CompilerParams(vmem_limit_bytes=VMEM_LIMIT),
        cost_estimate=pl.CostEstimate(
            flops=8 * edges * rows * width, bytes_accessed=8 * edges * width, transcendentals=0
        ),
        name="prepare_round",
    )(own, w, edge_src, negatives)


def round_kernel(
    r,
    batches,
    count_ref,
    mate_ref,
    w_ref,
    source_ref,
    product_ref,
    seen_ref,
    src_ref,
    dst_ref,
    src_grad,
    dst_grad,
    dw_ref,
):
    rows, width = mate_ref.shape
    half = width // 2
    edges = src_ref.shape[2]
    batch = edges // batches
    chunk = 2 * batch
    mate = mate_ref[...]
    total = count_ref[0, r]
    src_sum = dst_sum = None
    for c in range(edges // chunk):
        span = slice(c * chunk, (c + 1) * chunk)
        dst_mask = hot_columns(as_column(dst_ref[0, r : r + 1, span]), rows)
        source = source_ref[span, :].astype(f32)
        a_re, a_im = source[:, :half], source[:, half:]
        w = w_ref[span, :].astype(f32)
        w_re, w_im = w[:, :half], w[:, half:]
        u = product_ref[span, :]
        score = lax.dot_general(u, mate, (((1,), (1,)), ((), ())), preferred_element_type=f32)
        positive = jnp.sum(dst_mask * score, axis=1, keepdims=True)
        times = jnp.concatenate(
            [jnp.broadcast_to(seen_ref[b : b + 1, :], (batch, rows)) for b in (2 * c, 2 * c + 1)],
            axis=0,
        )
        slot = lax.broadcasted_iota(i32, (chunk, rows), 0) + c * chunk
        weight = jnp.where(slot < total, times, 0.0) * jax.nn.sigmoid(score - positive)
        pull = -jnp.sum(weight, axis=1, keepdims=True)
        weight = (weight + pull * dst_mask).astype(bf16)
        du = dot(weight, mate)
        part = lax.dot_general(weight, u, (((0,), (0,)), ((), ())), preferred_element_type=f32)
        dst_sum = part if dst_sum is None else dst_sum + part
        g_re, g_im = du[:, :half], du[:, half:]
        dw_ref[span, :] = jnp.concatenate(
            [g_re * a_re + g_im * a_im, g_im * a_re - g_re * a_im], axis=1
        ).astype(bf16)
        da = jnp.concatenate(
            [g_re * w_re + g_im * w_im, g_im * w_re - g_re * w_im], axis=1
        ).astype(bf16)
        part = dot(hot_rows(src_ref[0, r : r + 1, span], 0, rows), da)
        src_sum = part if src_sum is None else src_sum + part
    src_grad[...] = src_sum
    dst_grad[...] = dst_sum.astype(bf16)


def run_round(r, edge_counts, mate, w, ready, edge_src, edge_dst):
    rows, width = mate.shape
    edges = edge_src.shape[2]
    out = [
        jax.ShapeDtypeStruct((rows, width), f32),
        jax.ShapeDtypeStruct((rows, width), bf16),
        jax.ShapeDtypeStruct((edges, width), bf16),
    ]
    operands = (mate, w, *ready, edge_src, edge_dst)
    return pl.pallas_call(
        functools.partial(round_kernel, r, ready[2].shape[0]),
        grid=(1,),
        in_specs=[pl.BlockSpec(memory_space=pltpu.SMEM)] + [whole(x) for x in operands],
        out_specs=[whole(x) for x in out],
        out_shape=out,
        compiler_params=pltpu.CompilerParams(vmem_limit_bytes=VMEM_LIMIT),
        name="train_round",
    )(edge_counts, *operands)


def exchange(value, mask, beside=None, *operands):
    size = lax.axis_size("dom")

    def hop(m, value, *operands):
        came = lax.ppermute(value, "dom", [(i, i ^ m) for i in range(size)])
        return came if beside is None else (came, beside(*operands))

    hops = [functools.partial(hop, m) for m in range(1, size)]
    return lax.switch(mask - 1, hops, value, *operands)


def local(entities, relations, edge_src, edge_rel, edge_dst, negatives, plan, edge_counts):
    grad_total = jnp.zeros(entities.shape, f32)
    w, table = pick_relations(relations, edge_rel, 0, 256)
    dws = []
    rounds = plan.shape[0]
    for r in range(rounds):
        own = entities.astype(bf16)
        first = functools.partial(prepare, r=r)
        mate, ready = exchange(own, plan[r], first, own, w, edge_src, negatives)
        own_grad, mate_grad, dw = run_round(r, edge_counts, mate, w, ready, edge_src, edge_dst)
        dws.append(dw)
        if r + 1 < rounds:
            pick = functools.partial(pick_relations, r=r + 1, rows=256)
            back, w = exchange(mate_grad, plan[r], pick, table, edge_rel)
        else:
            back = exchange(mate_grad, plan[r])
        grad = own_grad + back.astype(f32)
        grad_total = grad_total + grad
        entities = entities - step_size * grad
    return grad_total, reduce_relations(edge_rel, dws, relations.shape[0])


def solution(mesh):
    both = ("grp", "dom")
    placed = (
        P(both, None),
        P(),
        P(both, None, None),
        P(both, None, None),
        P(both, None, None),
        P(both, None, None, None),
        P(),
        P(both, None),
    )
    return jax.shard_map(
        local,
        mesh=mesh,
        in_specs=placed,
        out_specs=(P(both, None), P("dom", None)),
        check_vma=False,
    )
```

```python
import functools

import jax
import jax.numpy as jnp
from jax import lax
from jax.experimental import pallas as pl
from jax.experimental.pallas import tpu as pltpu
from jax.sharding import PartitionSpec as P

step_size = 0.1
LANES = 128
VMEM_LIMIT = 48 * 1024 * 1024
MESH = pl.DeviceIdType.MESH
f32, bf16, i32 = jnp.float32, jnp.bfloat16, jnp.int32


def as_column(ids):
    return jnp.transpose(jnp.broadcast_to(ids, (LANES, ids.shape[1])))


def hot_columns(column, count):
    lane = lax.broadcasted_iota(i32, column.shape, 1)
    return jnp.concatenate(
        [jnp.where(column == lane + t, 1.0, 0.0) for t in range(0, count, LANES)], axis=1
    )


def hot_rows(ids, first, count):
    row = lax.broadcasted_iota(i32, (count, ids.shape[1]), 0) + first
    return jnp.where(row == ids, 1.0, 0.0).astype(bf16)


def dot(a, b):
    return jnp.dot(a, b, preferred_element_type=f32)


def pick_relations_kernel(r, rel_ref, ids_ref, out_ref, table_ref=None):
    c = pl.program_id(0)
    rows = out_ref.shape[0]
    if table_ref is not None:

        @pl.when(c == 0)
        def _():
            table_ref[...] = rel_ref[...].astype(bf16)

        rel_ref = table_ref

    ids = ids_ref[0, r : r + 1, pl.ds(pl.multiple_of(c * rows, rows), rows)]
    hot = hot_columns(as_column(ids), rel_ref.shape[0]).astype(bf16)
    out_ref[...] = dot(hot, rel_ref[...]).astype(bf16)


def pick_relations(relations, edge_rel, r, rows):
    edges = edge_rel.shape[2]
    rel, width = relations.shape
    table = pl.BlockSpec((rel, width), lambda c: (0, 0))
    wide = relations.dtype != bf16
    out = pl.pallas_call(
        functools.partial(pick_relations_kernel, r),
        grid=(edges // rows,),
        in_specs=[table, pl.BlockSpec(edge_rel.shape, lambda c: (0, 0, 0))],
        out_specs=[pl.BlockSpec((rows, width), lambda c: (c, 0))] + [table] * wide,
        out_shape=[jax.ShapeDtypeStruct((edges, width), bf16)]
        + [jax.ShapeDtypeStruct((rel, width), bf16)] * wide,
        compiler_params=pltpu.CompilerParams(vmem_limit_bytes=VMEM_LIMIT),
        cost_estimate=pl.CostEstimate(
            flops=2 * edges * rel * width, bytes_accessed=2 * (rel + edges) * width, transcendentals=0
        ),
        name="pick_relations",
    )(relations, edge_rel)
    return out if wide else out[0]


def reduce_relations_kernel(
    groups,
    size,
    stride,
    ids_ref,
    dw0,
    dw1,
    dw2,
    dw3,
    out_ref,
    own_sum,
    core_out,
    core_in,
    group_out,
    group_in,
    chip_out,
    chip_in,
    share_out,
    share_in,
    core_sems,
    group_sems,
    chip_sems,
    share_sems,
):
    g, d = lax.axis_index("grp"), lax.axis_index("dom")
    core, chip = lax.rem(d, 2), lax.div(d, 2)
    chips = size // 2
    pad = own_sum.shape[1]
    rows = pad // groups

    def flip(index, mask):
        bits = [lax.rem(lax.div(index, 1 << b), 2) for b in range(mask.bit_length())]
        return index + sum(
            ((1 - 2 * bit) << b for b, bit in enumerate(bits) if mask >> b & 1), jnp.int32(0)
        )

    mate = flip(d, 1)
    group_mates = [flip(g, k) for k in range(1, groups)]
    chip_mates = [flip(chip, k) for k in range(1, chips)]
    greet = [(g, mate)] + [(m, d) for m in group_mates] + [(g, 2 * m + core) for m in chip_mates]
    barrier = pltpu.get_barrier_semaphore()
    for device in greet:
        pl.semaphore_signal(barrier, inc=1, device_id=device, device_id_type=MESH)
    pl.semaphore_wait(barrier, len(greet))

    def send(source, target, sems, at, device):
        return pltpu.make_async_remote_copy(
            src_ref=source,
            dst_ref=target,
            send_sem=sems.at[(0,) + at],
            recv_sem=sems.at[(1,) + at],
            device_id=device,
            device_id_type=MESH,
        )

    def partial_sum(index):
        total = None
        for r, dw in enumerate((dw0, dw1, dw2, dw3)):
            part = dot(hot_rows(ids_ref[0, r : r + 1, :], index * stride, pad), dw[...])
            total = part if total is None else total + part
        return total

    def to_core(i):
        return send(core_out.at[i], core_in.at[i], core_sems, (i,), (g, mate))

    def to_group(i, k):
        m = group_mates[k]
        there = pl.ds(pl.multiple_of(m * rows, rows), rows)
        return send(
            group_out.at[i, there], group_in.at[k, i], group_sems, (k, i), (m, d)
        )

    def first(i, carry):
        core_out[i] = partial_sum(2 * i + 1 - core)
        to_core(i).start()
        return carry

    lax.fori_loop(0, chips, first, 0)

    def second(i, carry):
        own = partial_sum(2 * i + core)
        to_core(i).wait()
        own = own + core_in[i]
        own_sum[i] = own
        group_out[i] = own.astype(bf16)
        for k in range(groups - 1):
            to_group(i, k).start()
        return carry

    lax.fori_loop(0, chips, second, 0)
    here = pl.ds(pl.multiple_of(g * rows, rows), rows)

    def third(i, carry):
        total = own_sum[i, here]
        for k in range(groups - 1):
            to_group(i, k).wait()
            total = total + group_in[k, i].astype(f32)
        own_sum[i, here] = total
        chip_out[i] = total.astype(bf16)
        return carry

    lax.fori_loop(0, chips, third, 0)
    copies = [
        send(chip_out.at[m], chip_in.at[k], chip_sems, (k,), (g, 2 * m + core))
        for k, m in enumerate(chip_mates)
    ]
    for copy in copies:
        copy.start()
    total = own_sum[chip, here]
    for k, copy in enumerate(copies):
        copy.wait()
        total = total + chip_in[k].astype(f32)
    share_out[...] = total
    copies = [
        send(share_out, share_in.at[k], share_sems, (k,), (m, d))
        for k, m in enumerate(group_mates)
    ]
    for copy in copies:
        copy.start()
    out_ref[here, :] = share_out[...]
    for k, (copy, m) in enumerate(zip(copies, group_mates)):
        copy.wait()
        out_ref[pl.ds(pl.multiple_of(m * rows, rows), rows), :] = share_in[k]


def reduce_relations(edge_rel, dws, rel):
    width = dws[0].shape[1]
    groups, size = lax.axis_size("grp"), lax.axis_size("dom")
    chips = size // 2
    stride = rel // size
    rows = -(-stride // (16 * groups)) * 16
    pad = rows * groups
    whole = pl.BlockSpec(memory_space=pltpu.VMEM)
    dma = lambda *shape: pltpu.SemaphoreType.DMA((2,) + shape)
    out = pl.pallas_call(
        functools.partial(reduce_relations_kernel, groups, size, stride),
        in_specs=[whole] * (1 + len(dws)),
        out_specs=whole,
        out_shape=jax.ShapeDtypeStruct((pad, width), f32),
        scratch_shapes=[
            pltpu.VMEM((chips, pad, width), f32),
            pltpu.VMEM((chips, pad, width), f32),
            pltpu.VMEM((chips, pad, width), f32),
            pltpu.VMEM((chips, pad, width), bf16),
            pltpu.VMEM((groups - 1, chips, rows, width), bf16),
            pltpu.VMEM((chips, rows, width), bf16),
            pltpu.VMEM((chips - 1, rows, width), bf16),
            pltpu.VMEM((rows, width), f32),
            pltpu.VMEM((groups - 1, rows, width), f32),
            dma(chips),
            dma(groups - 1, chips),
            dma(chips - 1),
            dma(groups - 1),
        ],
        compiler_params=pltpu.CompilerParams(
            vmem_limit_bytes=VMEM_LIMIT, collective_id=0, has_side_effects=True
        ),
        name="reduce_relations",
    )(edge_rel, *dws)
    return out[:stride]


def round_kernel(
    r, count_ref, ent_ref, mate_ref, w_ref, src_ref, dst_ref, neg_ref, src_grad, dst_grad, dw_ref
):
    rows, width = ent_ref.shape
    half = width // 2
    edges = src_ref.shape[2]
    batches, negs = neg_ref.shape[2:]
    batch = edges // batches
    chunk = 2 * batch
    own = ent_ref[...].astype(bf16)
    mate = mate_ref[...]
    total = count_ref[0, r]
    ones = jnp.ones((8, negs), bf16)
    src_sum = dst_sum = None
    for c in range(edges // chunk):
        span = slice(c * chunk, (c + 1) * chunk)
        src_ids = src_ref[0, r : r + 1, span]
        dst_mask = hot_columns(as_column(dst_ref[0, r : r + 1, span]), rows)
        source = dot(hot_columns(as_column(src_ids), rows).astype(bf16), own)
        a_re, a_im = source[:, :half], source[:, half:]
        w = w_ref[span, :].astype(f32)
        w_re, w_im = w[:, :half], w[:, half:]
        u = jnp.concatenate(
            [a_re * w_re - a_im * w_im, a_re * w_im + a_im * w_re], axis=1
        ).astype(bf16)
        score = lax.dot_general(u, mate, (((1,), (1,)), ((), ())), preferred_element_type=f32)
        positive = jnp.sum(dst_mask * score, axis=1, keepdims=True)
        times = []
        for b in (2 * c, 2 * c + 1):
            hot = hot_rows(neg_ref[0, r, b : b + 1, :], 0, rows)
            seen = lax.dot_general(ones, hot, (((1,), (1,)), ((), ())), preferred_element_type=f32)
            times.append(jnp.broadcast_to(seen[:1], (batch, rows)))
        slot = lax.broadcasted_iota(i32, (chunk, rows), 0) + c * chunk
        times = jnp.where(slot < total, jnp.concatenate(times, axis=0) * (1.0 / negs), 0.0)
        weight = times * jax.nn.sigmoid(score - positive)
        pull = -jnp.sum(weight, axis=1, keepdims=True)
        weight = (weight + pull * dst_mask).astype(bf16)
        du = dot(weight, mate)
        part = lax.dot_general(weight, u, (((0,), (0,)), ((), ())), preferred_element_type=f32)
        dst_sum = part if dst_sum is None else dst_sum + part
        g_re, g_im = du[:, :half], du[:, half:]
        dw_ref[span, :] = jnp.concatenate(
            [g_re * a_re + g_im * a_im, g_im * a_re - g_re * a_im], axis=1
        ).astype(bf16)
        da = jnp.concatenate(
            [g_re * w_re + g_im * w_im, g_im * w_re - g_re * w_im], axis=1
        ).astype(bf16)
        part = dot(hot_rows(src_ids, 0, rows), da)
        src_sum = part if src_sum is None else src_sum + part
    src_grad[...] = src_sum
    dst_grad[...] = dst_sum.astype(bf16)


def run_round(r, edge_counts, entities, mate, w, edge_src, edge_dst, negatives):
    rows, width = entities.shape
    edges = edge_src.shape[2]
    whole = lambda x: pl.BlockSpec(x.shape, lambda i: (0,) * x.ndim)
    return pl.pallas_call(
        functools.partial(round_kernel, r),
        grid=(1,),
        in_specs=[
            pl.BlockSpec(memory_space=pltpu.SMEM),
            whole(entities),
            whole(mate),
            whole(w),
            whole(edge_src),
            whole(edge_dst),
            whole(negatives),
        ],
        out_specs=[
            pl.BlockSpec((rows, width), lambda i: (0, 0)),
            pl.BlockSpec((rows, width), lambda i: (0, 0)),
            pl.BlockSpec((edges, width), lambda i: (0, 0)),
        ],
        out_shape=[
            jax.ShapeDtypeStruct((rows, width), f32),
            jax.ShapeDtypeStruct((rows, width), bf16),
            jax.ShapeDtypeStruct((edges, width), bf16),
        ],
        compiler_params=pltpu.CompilerParams(vmem_limit_bytes=VMEM_LIMIT),
        name="train_round",
    )(edge_counts, entities, mate, w, edge_src, edge_dst, negatives)


def exchange(value, mask, beside=None, *operands):
    size = lax.axis_size("dom")

    def hop(m, value, *operands):
        came = lax.ppermute(value, "dom", [(i, i ^ m) for i in range(size)])
        return came if beside is None else (came, beside(*operands))

    hops = [functools.partial(hop, m) for m in range(1, size)]
    return lax.switch(mask - 1, hops, value, *operands)


def local(entities, relations, edge_src, edge_rel, edge_dst, negatives, plan, edge_counts):
    grad_total = jnp.zeros(entities.shape, f32)
    dws = []
    rounds = plan.shape[0]
    for r in range(rounds):
        own = entities.astype(bf16)
        if r == 0:
            pick = functools.partial(pick_relations, r=0, rows=256)
            mate, (w, table) = exchange(own, plan[0], pick, relations, edge_rel)
        else:
            mate = exchange(own, plan[r])
        own_grad, mate_grad, dw = run_round(
            r, edge_counts, entities, mate, w, edge_src, edge_dst, negatives
        )
        dws.append(dw)
        if r + 1 < rounds:
            pick = functools.partial(pick_relations, r=r + 1, rows=256)
            back, w = exchange(mate_grad, plan[r], pick, table, edge_rel)
        else:
            back = exchange(mate_grad, plan[r])
        grad = own_grad + back.astype(f32)
        grad_total = grad_total + grad
        entities = entities - step_size * grad
    return grad_total, reduce_relations(edge_rel, dws, relations.shape[0])


def solution(mesh):
    both = ("grp", "dom")
    placed = (
        P(both, None),
        P(),
        P(both, None, None),
        P(both, None, None),
        P(both, None, None),
        P(both, None, None, None),
        P(),
        P(both, None),
    )
    return jax.shard_map(
        local,
        mesh=mesh,
        in_specs=placed,
        out_specs=(P(both, None), P("dom", None)),
        check_vma=False,
    )
```
